32 devices in a mesh: dp: 8 (over y, x, core), tensor: 4 (over z).
Axes of the slice: x: 2, y: 2, z: 4, core: 2. Of those that a mesh axis runs over, the one named last changes fastest.
Arguments:
- hidden_states: bfloat16 [6144, 4096], P('dp', 'tensor')
- neighbour_ids: int32 [96, 2], P('dp'), may hold values from 0 to 127, as said below
- database: bfloat16 [128, 128, 896], P('dp')
- w_up: bfloat16 [896, 3584], P(None, 'tensor'), may hold values from -0.1875 to 0.1875
- w_down: bfloat16 [3584, 896], P('tensor'), may hold values from -0.09375 to 0.09375
- w_query: bfloat16 [4096, 4096], P(None, 'tensor'), may hold values from -0.09375 to 0.09375
- w_key: bfloat16 [896, 4096], P(None, 'tensor'), may hold values from -0.1875 to 0.1875
- w_value: bfloat16 [896, 4096], P(None, 'tensor'), may hold values from -0.1875 to 0.1875
Outputs:
- attended: bfloat16 [6144, 4096], P('dp', 'tensor')
The draws below stay inside these ranges and needn't reach their ends.
Inputs may be any that keep to these rules, and one draw needn't show every extreme that they name: `neighbour_ids`: block ids are grouped by owner: index s of dp holds blocks s * 16 to (s + 1) * 16 - 1. Among the 24 ids of one sequence, no owner's blocks are named more than 4 times; one owner, the same for every sequence, is named exactly 4 times by each.
All inputs are finite; a program needn't handle non-finite values.
Results may differ from the reference program's by a relative error of at most 0.02.
Values may be sent and summed in bfloat16 or wider, within the bound.
A program may use at most 128 MiB of HBM per device.

```python
import math
import jax
import jax.numpy as jnp
from jax import lax

D = 4096
HEADS = 32
HD = 128
E = 896
FF = 3584
SPAN = 64
KN = 2
NTOK = 128
CH = 12
DB_DEV = 16
SEQ = 768
TOKENS = 6144
SPANS = 96
DB = 128
CAP = 4
N_DP = 8
N_TENSOR = 4


def scaled_field(key, shape):
    key_base, key_rows, key_cols = jax.random.split(key, 3)
    row_shape = shape[:-1] + (1,)
    col_shape = (1,) * (len(shape) - 1) + (shape[-1],)
    rows_scale = jnp.exp(jax.random.uniform(key_rows, row_shape, jnp.float32, math.log(0.3), math.log(3.0)))
    cols_scale = jnp.exp(jax.random.uniform(key_cols, col_shape, jnp.float32, math.log(0.3), math.log(3.0)))
    base = jnp.clip(jax.random.normal(key_base, shape, jnp.float32), -4.0, 4.0)
    return base * rows_scale * cols_scale


def draw_hidden_states(key, part):
    return scaled_field(key, (TOKENS, D)).astype(jnp.bfloat16)


def draw_database(key, part):
    return scaled_field(key, (DB, NTOK, E)).astype(jnp.bfloat16)


def draw_neighbour_ids(key, part):
    key_hot, key_blocks, key_local = jax.random.split(jax.random.fold_in(key, 7), 3)
    request_count = CH * KN
    favourite = jax.random.randint(key_hot, (), 0, N_DP)

    def one_block(block_key):
        key_order, key_rest, key_mix = jax.random.split(block_key, 3)
        order = jax.random.permutation(key_order, N_DP)
        order = order[jnp.argsort((order != favourite).astype(jnp.int32), stable=True)]
        owner_pool = jnp.repeat(order, CAP)
        remainder = jax.random.permutation(key_rest, owner_pool[CAP:])
        chosen = jnp.concatenate([owner_pool[:CAP], remainder])[:request_count]
        return jax.random.permutation(key_mix, chosen)
    owners = jax.vmap(one_block)(jax.random.split(key_blocks, N_DP))
    local_rows = jax.random.randint(key_local, (N_DP, request_count), 0, DB_DEV)
    return (owners * DB_DEV + local_rows).reshape(SPANS, KN).astype(jnp.int32)


def block_levels(rng, dims, pieces, smallest, largest):
    gain = 1.0
    for dim, blocks in pieces:
        draws = jax.random.uniform(jax.random.fold_in(jax.random.fold_in(rng, 6), dim), (blocks,), jnp.float32, smallest / len(pieces), largest / len(pieces))
        gain = gain * jnp.repeat(jnp.exp(draws), dims[dim] // blocks).reshape((-1,) + (1,) * (len(dims) - 1 - dim))
    return gain


def centred(own_key, shape, spread, limit, cuts=(), held_as=jnp.bfloat16):
    loudness = block_levels(own_key, shape, cuts, -0.22, 0.18) if cuts else 1.0
    values = jax.random.normal(own_key, shape, jnp.float32) * spread * loudness
    return jnp.minimum(jnp.maximum(values, -limit), limit).astype(held_as)


def setup_inputs(seed: int = 0) -> dict:
    arg_keys = jax.random.split(jax.random.key(seed), 9)
    hidden_states = draw_hidden_states(jax.random.fold_in(arg_keys[8], 71), 0)
    neighbour_ids = draw_neighbour_ids(jax.random.fold_in(arg_keys[8], 71), 0)
    database = draw_database(jax.random.fold_in(arg_keys[8], 71), 0)
    w_up = centred(arg_keys[3], (E, FF), E ** -0.5, 0.1875, ((1, 4),))
    w_down = centred(arg_keys[4], (FF, E), FF ** -0.5, 0.09375, ((0, 4),))
    w_query = centred(arg_keys[5], (D, D), D ** -0.5, 0.09375, ((1, 4),))
    w_key = centred(arg_keys[6], (E, D), E ** -0.5, 0.1875, ((1, 4),))
    w_value = centred(arg_keys[7], (E, D), E ** -0.5, 0.1875, ((1, 4),))
    return dict(hidden_states=hidden_states, neighbour_ids=neighbour_ids, database=database, w_up=w_up, w_down=w_down, w_query=w_query, w_key=w_key, w_value=w_value)


EPSILON = 1e-06
LOGIT_SCALE = 3.0

def head_norm(projected):
    shaped = projected.reshape(projected.shape[0], -1, HD)
    scaled = shaped * lax.rsqrt(lax.optimization_barrier(jnp.mean(shaped * shaped, axis=-1, keepdims=True)) + EPSILON)
    return scaled.astype(jnp.bfloat16)

def attend(queries, keys, values):
    seq_rows = queries.shape[0]
    heads_here = queries.shape[1]
    span_count = seq_rows // SPAN
    shifted = jnp.concatenate([queries[SPAN - 1:], jnp.zeros((SPAN - 1, heads_here, HD), jnp.bfloat16)], axis=0)
    windows = shifted.reshape(span_count, SPAN, heads_here, HD)
    key_blocks = keys.reshape(span_count, KN * NTOK, heads_here, HD)
    value_blocks = values.reshape(span_count, KN * NTOK, heads_here, HD)
    scores = jnp.einsum('cqhd,ckhd->chqk', windows.astype(jnp.float32), key_blocks.astype(jnp.float32))
    scores = scores * (LOGIT_SCALE / math.sqrt(HD))
    expo = jnp.exp(scores)
    weights = (expo / lax.optimization_barrier(jnp.sum(expo, axis=-1, keepdims=True))).astype(jnp.bfloat16)
    mixed = jnp.einsum('chqk,ckhd->cqhd', weights.astype(jnp.float32), value_blocks.astype(jnp.float32))
    mixed = mixed.astype(jnp.bfloat16).reshape(seq_rows, heads_here * HD)
    leading = jnp.zeros((SPAN - 1, heads_here * HD), jnp.bfloat16)
    return jnp.concatenate([leading, mixed[:seq_rows - SPAN + 1]], axis=0)

def reference(hidden_states, neighbour_ids, database, w_up, w_down, w_query, w_key, w_value):

    def one_sequence(operands):
        states, chosen = operands
        blocks = database[chosen.reshape(-1)]
        raw_float = blocks.astype(jnp.float32)
        normed = (raw_float * lax.rsqrt(lax.optimization_barrier(jnp.mean(raw_float * raw_float, axis=-1, keepdims=True)) + EPSILON)).astype(jnp.bfloat16)
        inner = jnp.einsum('bte,ef->btf', normed.astype(jnp.float32), w_up.astype(jnp.float32))
        active = jax.nn.gelu(inner).astype(jnp.bfloat16)
        grouped = active.reshape(active.shape[0], NTOK, N_TENSOR, FF // N_TENSOR)
        down_grouped = w_down.reshape(N_TENSOR, FF // N_TENSOR, E)
        partials = jnp.einsum('btgf,gfe->gbte', grouped.astype(jnp.float32), down_grouped.astype(jnp.float32))
        partials = lax.optimization_barrier(partials.astype(jnp.bfloat16)).astype(jnp.float32)
        encoded = (raw_float + lax.optimization_barrier(jnp.sum(partials, axis=0))).astype(jnp.bfloat16)
        flat_encoded = encoded.reshape(-1, E)
        keys = head_norm(jnp.dot(flat_encoded, w_key, preferred_element_type=jnp.float32))
        values = jnp.dot(flat_encoded, w_value, preferred_element_type=jnp.float32).astype(jnp.bfloat16)
        values = values.reshape(flat_encoded.shape[0], HEADS, HD)
        queries = head_norm(jnp.dot(states, w_query, preferred_element_type=jnp.float32))
        return attend(queries, keys, values)
    states_all = hidden_states.reshape(N_DP, SEQ, D)
    chosen_all = neighbour_ids.reshape(N_DP, CH, KN)
    result = lax.map(one_sequence, (states_all, chosen_all))
    return result.reshape(TOKENS, D)
```

```python
import functools
import math

import jax
import jax.numpy as jnp
from jax import lax
from jax.experimental import pallas as pl
from jax.experimental.pallas import tpu as pltpu
from jax.sharding import PartitionSpec as P

HD = 128
SPAN = 64
KN = 2
NTOK = 128

EPSILON = 1e-06
LOGIT_SCALE = 3.0
PARTS = 2
GROUP = 4
MIB = 1024 * 1024


def pick_kernel(parts, ids_ref, block_ref, *out_refs):
    rows = block_ref.shape[1] // parts
    for part in range(parts):
        out_refs[part][...] = block_ref[:, part * rows : (part + 1) * rows, :]


def pick_blocks(ids, database, parts):
    count = ids.shape[0]
    _, tokens, width = database.shape
    rows = tokens // parts
    return pl.pallas_call(
        functools.partial(pick_kernel, parts),
        grid_spec=pltpu.PrefetchScalarGridSpec(
            num_scalar_prefetch=1,
            grid=(count,),
            in_specs=[pl.BlockSpec((1, tokens, width), lambda i, ids_ref: (ids_ref[i], 0, 0))],
            out_specs=[pl.BlockSpec((1, rows, width), lambda i, ids_ref: (i, 0, 0))] * parts,
        ),
        out_shape=[jax.ShapeDtypeStruct((count, rows, width), database.dtype)] * parts,
        cost_estimate=pl.CostEstimate(
            flops=0, bytes_accessed=4 * count * tokens * width, transcendentals=0
        ),
    )(ids, database)


def encode_kernel(slots_ref, *refs):
    blocks = refs[:GROUP]
    up_ref, down_ref, key_ref, value_ref, keys_ref, values_ref = refs[GROUP:]
    raw = jnp.concatenate([ref[0] for ref in blocks], axis=0).astype(jnp.float32)
    normed = (
        raw * lax.rsqrt(jnp.mean(raw * raw, axis=-1, keepdims=True) + EPSILON)
    ).astype(jnp.bfloat16)
    total = raw
    for g in range(up_ref.shape[0]):
        inner = jnp.dot(normed, up_ref[g], preferred_element_type=jnp.float32)
        active = jax.nn.gelu(inner).astype(jnp.bfloat16)
        total = total + jnp.dot(active, down_ref[g], preferred_element_type=jnp.float32)
    encoded = total.astype(jnp.bfloat16)
    rows = blocks[0].shape[1]
    keys = jnp.dot(encoded, key_ref[...], preferred_element_type=jnp.float32)
    for h in range(keys.shape[1] // HD):
        cols = slice(h * HD, (h + 1) * HD)
        head = keys[:, cols]
        head = head * lax.rsqrt(jnp.mean(head * head, axis=-1, keepdims=True) + EPSILON)
        keys_ref[:, :, cols] = head.astype(jnp.bfloat16).reshape(GROUP, rows, HD)
    values = jnp.dot(encoded, value_ref[...], preferred_element_type=jnp.float32)
    values_ref[...] = values.astype(jnp.bfloat16).reshape(values_ref.shape)


def encode(slots, blocks, up, down, w_key, w_value):
    count = slots.shape[0]
    _, rows, width = blocks.shape
    columns = w_key.shape[1]
    hidden = up.shape[0] * up.shape[2]

    def whole(array):
        return pl.BlockSpec(array.shape, lambda i, slots_ref, n=array.ndim: (0,) * n)

    block_specs = [
        pl.BlockSpec((1, rows, width), lambda i, slots_ref, j=j: (slots_ref[i * GROUP + j], 0, 0))
        for j in range(GROUP)
    ]
    out_spec = pl.BlockSpec((GROUP, rows, columns), lambda i, slots_ref: (i, 0, 0))
    return pl.pallas_call(
        encode_kernel,
        grid_spec=pltpu.PrefetchScalarGridSpec(
            num_scalar_prefetch=1,
            grid=(count // GROUP,),
            in_specs=block_specs + [whole(a) for a in (up, down, w_key, w_value)],
            out_specs=[out_spec, out_spec],
        ),
        out_shape=[jax.ShapeDtypeStruct((count, rows, columns), jnp.bfloat16)] * 2,
        compiler_params=pltpu.CompilerParams(vmem_limit_bytes=56 * MIB),
        cost_estimate=pl.CostEstimate(
            flops=4 * count * rows * width * (hidden + columns),
            bytes_accessed=2 * (count * rows * (width + 2 * columns) + 2 * width * (hidden + columns)),
            transcendentals=count * rows * hidden,
        ),
    )(slots, *([blocks] * GROUP), up, down, w_key, w_value)


def attend_kernel(parts, queries_ref, *refs):
    keys = jnp.concatenate([r[...].reshape(-1, r.shape[2]) for r in refs[:parts]], axis=0)
    values = jnp.concatenate([r[...].reshape(-1, r.shape[2]) for r in refs[parts : 2 * parts]], axis=0)
    out_ref = refs[2 * parts]
    for h in range(queries_ref.shape[1] // HD):
        cols = slice(h * HD, (h + 1) * HD)
        scores = lax.dot_general(
            queries_ref[:, cols],
            keys[:, cols],
            (((1,), (1,)), ((), ())),
            preferred_element_type=jnp.float32,
        )
        expo = jnp.exp(scores * (LOGIT_SCALE / math.sqrt(HD)))
        weights = (expo / jnp.sum(expo, axis=-1, keepdims=True)).astype(jnp.bfloat16)
        out_ref[:, cols] = jnp.dot(
            weights, values[:, cols], preferred_element_type=jnp.float32
        ).astype(jnp.bfloat16)


def attend(windows, keys, values):
    rows, columns = windows.shape
    parts = len(keys)
    span = pl.BlockSpec((SPAN, columns), lambda i: (i, 0))
    kv = pl.BlockSpec((KN, keys[0].shape[1], columns), lambda i: (i, 0, 0))
    return pl.pallas_call(
        functools.partial(attend_kernel, parts),
        grid=(rows // SPAN,),
        in_specs=[span] + [kv] * (2 * parts),
        out_specs=span,
        out_shape=jax.ShapeDtypeStruct((rows, columns), jnp.bfloat16),
        cost_estimate=pl.CostEstimate(
            flops=4 * rows * KN * NTOK * columns,
            bytes_accessed=4 * rows * columns * (1 + KN * NTOK // SPAN),
            transcendentals=rows * KN * NTOK * columns // HD,
        ),
    )(windows, *keys, *values)


def head_norm(projected):
    shaped = projected.reshape(projected.shape[0], -1, HD)
    scaled = shaped * lax.rsqrt(jnp.mean(shaped * shaped, axis=-1, keepdims=True) + EPSILON)
    return scaled.astype(jnp.bfloat16).reshape(projected.shape)


def gather_pieces(mine):
    dp_count = lax.axis_size("dp")
    column = lax.all_gather(mine, "tensor")
    same_core = [list(range(core, dp_count, 2)) for core in range(2)]
    chip = [[2 * k, 2 * k + 1] for k in range(dp_count // 2)]
    half = lax.all_gather(column, "dp", axis_index_groups=same_core)
    full = lax.all_gather(half, "dp", axis_index_groups=chip)
    full = full.transpose(3, 2, 1, 0, 4, 5)
    return full.reshape(full.shape[:2] + (-1, full.shape[5]))


def own_piece(weight):
    piece = weight.shape[0] // lax.axis_size("dp")
    return lax.dynamic_slice_in_dim(weight, lax.axis_index("dp") * piece, piece, 0)


def gather_weights(w_up, w_down):
    up, down = own_piece(w_up), own_piece(w_down)
    if up.shape == down.shape:
        both = gather_pieces(jnp.stack([up, down]))
        return both[0], both[1]
    return gather_pieces(up[None])[0], gather_pieces(down[None])[0]


def shards(hidden_states, neighbour_ids, database, w_up, w_down, w_query, w_key, w_value):
    dp_count = lax.axis_size("dp")
    shard_blocks = database.shape[0]
    flat_ids = neighbour_ids.reshape(-1)
    request_count = flat_ids.shape[0]
    capacity = max(2, (request_count + dp_count - 1) // dp_count + 1)
    owners = flat_ids // shard_blocks
    local_rows = flat_ids % shard_blocks
    owner_match = (owners[:, None] == jnp.arange(dp_count, dtype=jnp.int32)[None, :]).astype(
        jnp.int32
    )
    positions = jnp.arange(request_count, dtype=jnp.int32)
    earlier = (positions[:, None] > positions[None, :]).astype(jnp.int32)
    ranks = jnp.sum(jnp.dot(earlier, owner_match) * owner_match, axis=1)
    slots = owners * capacity + ranks
    slot_match = slots[None, :] == jnp.arange(dp_count * capacity, dtype=jnp.int32)[:, None]
    requests = jnp.sum(jnp.where(slot_match, local_rows[None, :], 0), axis=1)
    requests = requests.reshape(dp_count, capacity)
    wanted = lax.all_to_all(requests, "dp", split_axis=0, concat_axis=0, tiled=True).reshape(-1)
    up, down = gather_weights(w_up, w_down)
    picked = pick_blocks(wanted, database, PARTS)
    states = lax.all_gather(hidden_states, "tensor", axis=1, tiled=True)
    keys, values = [], []
    for part in picked:
        received = lax.all_to_all(part, "dp", split_axis=0, concat_axis=0, tiled=True)
        part_keys, part_values = encode(slots, received, up, down, w_key, w_value)
        keys.append(part_keys)
        values.append(part_values)
    queries = head_norm(jnp.dot(states, w_query, preferred_element_type=jnp.float32))
    seq_rows, columns = queries.shape
    leading = jnp.zeros((SPAN - 1, columns), jnp.bfloat16)
    windows = jnp.concatenate([queries[SPAN - 1 :], leading], axis=0)
    mixed = attend(windows, keys, values)
    return jnp.concatenate([leading, mixed[: seq_rows - SPAN + 1]], axis=0)


def solution(mesh):
    in_specs = (
        P("dp", "tensor"),
        P("dp", None),
        P("dp", None, None),
        P(None, "tensor"),
        P("tensor", None),
        P(None, "tensor"),
        P(None, "tensor"),
        P(None, "tensor"),
    )
    out_specs = P("dp", "tensor")
    return jax.shard_map(shards, mesh=mesh, in_specs=in_specs, out_specs=out_specs, check_vma=False)
```

```python
import functools
import math

import jax
import jax.numpy as jnp
from jax import lax
from jax.experimental import pallas as pl
from jax.experimental.pallas import tpu as pltpu
from jax.sharding import PartitionSpec as P

HD = 128
SPAN = 64
KN = 2
NTOK = 128

EPSILON = 1e-06
LOGIT_SCALE = 3.0
GROUP = 4
PICK = 4
MIB = 1024 * 1024


def pick_kernel(ids_ref, *refs):
    out_ref = refs[-1]
    for j in range(PICK):
        out_ref[j] = refs[j][0]


def pick_blocks(ids, database):
    count = ids.shape[0]
    _, tokens, width = database.shape
    in_specs = [
        pl.BlockSpec((1, tokens, width), lambda i, ids_ref, j=j: (ids_ref[i * PICK + j], 0, 0))
        for j in range(PICK)
    ]
    return pl.pallas_call(
        pick_kernel,
        grid_spec=pltpu.PrefetchScalarGridSpec(
            num_scalar_prefetch=1,
            grid=(count // PICK,),
            in_specs=in_specs,
            out_specs=pl.BlockSpec((PICK, tokens, width), lambda i, ids_ref: (i, 0, 0)),
        ),
        out_shape=jax.ShapeDtypeStruct((count, tokens, width), database.dtype),
        cost_estimate=pl.CostEstimate(
            flops=0, bytes_accessed=4 * count * tokens * width, transcendentals=0
        ),
    )(ids, *([database] * PICK))


def gelu(x):
    half = 0.5 * x
    root = math.sqrt(2.0 / math.pi)
    return half + half * jnp.tanh(x * (root + (root * 0.044715) * (x * x)))


def encode_kernel(slots_ref, *refs):
    blocks = refs[:GROUP]
    windows_ref, up_ref, down_ref, key_ref, value_ref, out_ref = refs[GROUP:]
    raw = jnp.concatenate([ref[0] for ref in blocks], axis=0).astype(jnp.float32)
    normed = (
        raw * lax.rsqrt(jnp.mean(raw * raw, axis=-1, keepdims=True) + EPSILON)
    ).astype(jnp.bfloat16)
    total = raw
    for g in range(up_ref.shape[0]):
        inner = jnp.dot(normed, up_ref[g], preferred_element_type=jnp.float32)
        active = gelu(inner).astype(jnp.bfloat16)
        total = total + jnp.dot(active, down_ref[g], preferred_element_type=jnp.float32)
    encoded = total.astype(jnp.bfloat16)
    keys = jnp.dot(encoded, key_ref[...], preferred_element_type=jnp.float32)
    values = jnp.dot(encoded, value_ref[...], preferred_element_type=jnp.float32)
    values = values.astype(jnp.bfloat16)
    span_rows = KN * blocks[0].shape[1]
    for h in range(keys.shape[1] // HD):
        cols = slice(h * HD, (h + 1) * HD)
        head = keys[:, cols]
        head = head * lax.rsqrt(jnp.mean(head * head, axis=-1, keepdims=True) + EPSILON)
        head = head.astype(jnp.bfloat16)
        for c in range(GROUP // KN):
            rows = slice(c * span_rows, (c + 1) * span_rows)
            tokens = slice(c * SPAN, (c + 1) * SPAN)
            scores = lax.dot_general(
                windows_ref[tokens, cols],
                head[rows],
                (((1,), (1,)), ((), ())),
                preferred_element_type=jnp.float32,
            )
            expo = jnp.exp(scores * (LOGIT_SCALE / math.sqrt(HD)))
            weights = (expo / jnp.sum(expo, axis=-1, keepdims=True)).astype(jnp.bfloat16)
            out_ref[tokens, cols] = jnp.dot(
                weights, values[rows, cols], preferred_element_type=jnp.float32
            ).astype(jnp.bfloat16)


def encode_and_attend(slots, blocks, windows, up, down, w_key, w_value):
    count = slots.shape[0]
    _, rows, width = blocks.shape
    seq_rows, columns = windows.shape
    hidden = up.shape[0] * up.shape[2]

    def whole(array):
        return pl.BlockSpec(array.shape, lambda i, slots_ref, n=array.ndim: (0,) * n)

    block_specs = [
        pl.BlockSpec((1, rows, width), lambda i, slots_ref, j=j: (slots_ref[i * GROUP + j], 0, 0))
        for j in range(GROUP)
    ]
    window_spec = pl.BlockSpec((GROUP // KN * SPAN, columns), lambda i, slots_ref: (i, 0))
    return pl.pallas_call(
        encode_kernel,
        grid_spec=pltpu.PrefetchScalarGridSpec(
            num_scalar_prefetch=1,
            grid=(count // GROUP,),
            in_specs=block_specs + [window_spec] + [whole(a) for a in (up, down, w_key, w_value)],
            out_specs=window_spec,
        ),
        out_shape=jax.ShapeDtypeStruct((seq_rows, columns), jnp.bfloat16),
        compiler_params=pltpu.CompilerParams(vmem_limit_bytes=60 * MIB),
        cost_estimate=pl.CostEstimate(
            flops=4 * count * rows * width * (hidden + columns),
            bytes_accessed=2 * (count * rows * width + 2 * seq_rows * columns)
            + 4 * width * (hidden + columns),
            transcendentals=count * rows * hidden,
        ),
    )(slots, *([blocks] * GROUP), windows, up, down, w_key, w_value)


def head_norm(projected):
    shaped = projected.reshape(projected.shape[0], -1, HD)
    scaled = shaped * lax.rsqrt(jnp.mean(shaped * shaped, axis=-1, keepdims=True) + EPSILON)
    return scaled.astype(jnp.bfloat16).reshape(projected.shape)


def pass_along(low, high):
    n = lax.axis_size("tensor")
    up = [(i, i + 1) for i in range(n - 1)]
    down = [(i + 1, i) for i in range(n - 1)]
    return lax.ppermute(low, "tensor", up), lax.ppermute(high, "tensor", down)


def project_queries(from_low, from_high, w_query):
    n = lax.axis_size("tensor")
    here = lax.axis_index("tensor")
    depth = from_low[0].shape[1]
    projected = 0.0
    for m in range(n):
        shard = from_low[0]
        if m:
            shard = jnp.where(here + m < n, from_high[m], from_low[n - m])
        rows = lax.dynamic_slice_in_dim(w_query, (here + m) % n * depth, depth, 0)
        projected = projected + jnp.dot(shard, rows, preferred_element_type=jnp.float32)
    return head_norm(projected)


def gather_pieces(mine):
    return lax.all_gather(mine, "tensor")


def gather_cores(column):
    same_core = [list(range(core, lax.axis_size("dp"), 2)) for core in range(2)]
    return lax.all_gather(column, "dp", axis_index_groups=same_core)


def gather_chip(half):
    chip = [[2 * k, 2 * k + 1] for k in range(lax.axis_size("dp") // 2)]
    full = lax.all_gather(half, "dp", axis_index_groups=chip)
    full = full.transpose(3, 2, 1, 0, 4, 5)
    return full.reshape(full.shape[:2] + (-1, full.shape[5]))


def own_piece(weight):
    piece = weight.shape[0] // lax.axis_size("dp")
    return lax.dynamic_slice_in_dim(weight, lax.axis_index("dp") * piece, piece, 0)


def gather_columns(w_up, w_down):
    up, down = own_piece(w_up), own_piece(w_down)
    if up.shape == down.shape:
        return [gather_pieces(jnp.stack([up, down]))]
    return [gather_pieces(up[None]), gather_pieces(down[None])]


def shards(hidden_states, neighbour_ids, database, w_up, w_down, w_query, w_key, w_value):
    dp_count = lax.axis_size("dp")
    shard_blocks = database.shape[0]
    flat_ids = neighbour_ids.reshape(-1)
    request_count = flat_ids.shape[0]
    capacity = max(2, (request_count + dp_count - 1) // dp_count + 1)
    owners = flat_ids // shard_blocks
    local_rows = flat_ids % shard_blocks
    owner_match = (owners[:, None] == jnp.arange(dp_count, dtype=jnp.int32)[None, :]).astype(
        jnp.int32
    )
    positions = jnp.arange(request_count, dtype=jnp.int32)
    earlier = (positions[:, None] > positions[None, :]).astype(jnp.int32)
    ranks = jnp.sum(jnp.dot(earlier, owner_match) * owner_match, axis=1)
    slots = owners * capacity + ranks
    slot_match = slots[None, :] == jnp.arange(dp_count * capacity, dtype=jnp.int32)[:, None]
    requests = jnp.sum(jnp.where(slot_match, local_rows[None, :], 0), axis=1)
    requests = requests.reshape(dp_count, capacity)
    wanted = lax.all_to_all(requests, "dp", split_axis=0, concat_axis=0, tiled=True).reshape(-1)
    picked = pick_blocks(wanted, database)
    columns = gather_columns(w_up, w_down)
    first = pass_along(hidden_states, hidden_states)
    picked, columns, first = lax.optimization_barrier((picked, columns, first))
    received = lax.all_to_all(picked, "dp", split_axis=0, concat_axis=0, tiled=True)
    from_low, from_high = [hidden_states, first[0]], [hidden_states, first[1]]
    for _ in range(2, lax.axis_size("tensor")):
        low, high = pass_along(from_low[-1], from_high[-1])
        from_low.append(low)
        from_high.append(high)
    halves = [gather_cores(column) for column in columns]
    halves, received, from_low, from_high = lax.optimization_barrier(
        (halves, received, from_low, from_high)
    )
    up, down = [weight for half in halves for weight in gather_chip(half)]
    queries = project_queries(from_low, from_high, w_query)
    seq_rows = queries.shape[0]
    leading = jnp.zeros((SPAN - 1, queries.shape[1]), jnp.bfloat16)
    windows = jnp.concatenate([queries[SPAN - 1 :], leading], axis=0)
    mixed = encode_and_attend(slots, received, windows, up, down, w_key, w_value)
    return jnp.concatenate([leading, mixed[: seq_rows - SPAN + 1]], axis=0)


def solution(mesh):
    in_specs = (
        P("dp", "tensor"),
        P("dp", None),
        P("dp", None, None),
        P(None, "tensor"),
        P("tensor", None),
        P(None, "tensor"),
        P(None, "tensor"),
        P(None, "tensor"),
    )
    out_specs = P("dp", "tensor")
    return jax.shard_map(shards, mesh=mesh, in_specs=in_specs, out_specs=out_specs, check_vma=False)
```
